32 devices in a mesh: org: 4 (over x, core), dst: 8 (over z, y).
Axes of the slice: x: 2, y: 2, z: 4, core: 2. Of those that a mesh axis runs over, the one named last changes fastest.
Arguments:
- anchor_coords: float32 [2, 2048], P(None, 'org'), may hold values from 0 to 1
- dest_coords: float32 [2, 4096], P(None, 'dst'), may hold values from 0 to 1
- hour_decay: float32 [8], replicated, may hold values from 16 to 64
- anchor_district: int32 [2048], P('org'), may hold values from 0 to 511, as said below
- dest_district: int32 [4096], P('dst'), may hold values from 0 to 511, as said below
- anchor_target: float32 [8, 2048], P(None, 'org'), may hold values from 0.5 to 2
- dest_target: float32 [8, 4096], P(None, 'dst'), may hold values from 0.5 to 2
- pair_share: float32 [512, 512], replicated, may hold values from 0.5 to 2
- catchment: int32 [256, 512], P('org', 'dst'), may hold values from 0 to 1023
Outputs:
- pair_factor: float32 [512, 512], replicated
- anchor_factor: float32 [8, 2048], P(None, 'org')
- dest_factor: float32 [8, 4096], P(None, 'dst')
- lane_flows: float32 [8, 1024], P(None, ('org', 'dst'))
The draws below stay inside these ranges and needn't reach their ends.
Inputs may be any that keep to these rules, and one draw needn't show every extreme that they name: `anchor_district`: every district holds exactly 4 anchor zones. `dest_district`: every district holds exactly 8 destination zones.
All inputs are finite; a program needn't handle non-finite values.
Results may differ from the reference program's by a relative error of at most 0.00012.
Values sent between devices are 32-bit elements; how exact they have to be, the bound alone decides.
A program may use at most 128 MiB of HBM per device.

```python
import math
import jax
import jax.numpy as jnp
import numpy as np

H = 8
DIST = 512
TB = 8
SWEEPS = 2
ANCHORS = 2048
DESTS = 4096
LANES = 1024


def draw_anchor_district(key, part):
    key = jax.random.fold_in(key, 11)
    return (jax.random.permutation(key, ANCHORS) % DIST).astype(jnp.int32)


def draw_dest_district(key, part):
    key = jax.random.fold_in(key, 23)
    return (jax.random.permutation(key, DESTS) % DIST).astype(jnp.int32)


def set_ends(result, rng, least, largest):
    spot = [jax.random.randint(jax.random.fold_in(rng, axis), (), 0, length) for axis, length in enumerate(result.shape)]
    longest = result.shape.index(max(result.shape))
    beside = spot[:longest] + [(spot[longest] + 1) % result.shape[longest]] + spot[longest + 1:]
    return result.at[tuple(spot)].set(least).at[tuple(beside)].set(largest)


def block_scale(key, dims, shards, smallest, largest):
    gain = 1.0
    for axis_at, blocks in shards:
        draws = jax.random.uniform(jax.random.fold_in(jax.random.fold_in(key, 6), axis_at), (blocks,), jnp.float32, smallest / len(shards), largest / len(shards))
        gain = gain * jnp.repeat(jnp.exp(draws), dims[axis_at] // blocks).reshape((-1,) + (1,) * (len(dims) - 1 - axis_at))
    return gain


def rank_table(count, skew):
    loads = [(1 << 20) // math.isqrt(standing ** skew) + 1 for standing in range(1, count + 1)]
    scale = 1 + sum(loads) // (1 << 30)
    return np.cumsum(np.array([max(1, weight // scale) for weight in loads]))


def ranked_ids(own_key, dims, number_of, slope):
    table = rank_table(number_of, slope)
    ticket = jax.random.randint(jax.random.fold_in(own_key, 1), dims, 0, int(table[number_of - 1]))
    standing = jnp.searchsorted(jnp.asarray(table, jnp.int32), ticket, side="right")
    return jax.random.permutation(jax.random.fold_in(own_key, 2), number_of)[standing].astype(jnp.int32)


def setup_inputs(seed: int = 0) -> dict:
    seeds = jax.random.split(jax.random.key(seed), 10)
    return {
        "anchor_coords": jnp.clip(1.0 * jax.random.uniform(seeds[0], (2, ANCHORS), jnp.float32) ** block_scale(seeds[0], (2, ANCHORS), ((1, 4),), -0.2, 0.2), 0.0, 1.0),
        "dest_coords": jnp.clip(1.0 * jax.random.uniform(seeds[1], (2, DESTS), jnp.float32) ** block_scale(seeds[1], (2, DESTS), ((1, 8),), -0.2, 0.2), 0.0, 1.0),
        "hour_decay": jnp.clip(jnp.exp(jax.random.uniform(seeds[2], (H,), jnp.float32, math.log(16.0), math.log(64.0))), 16.0, 64.0),
        "anchor_district": draw_anchor_district(jax.random.fold_in(seeds[9], 71), 0),
        "dest_district": draw_dest_district(jax.random.fold_in(seeds[9], 71), 0),
        "anchor_target": jnp.clip(jnp.exp(math.log(2.0) - 1.3862944 * jax.random.uniform(seeds[5], (H, ANCHORS), jnp.float32) ** block_scale(seeds[5], (H, ANCHORS), ((1, 4),), -0.2, 0.2)), 0.5, 2.0),
        "dest_target": jnp.clip(jnp.exp(math.log(2.0) - 1.3862944 * jax.random.uniform(seeds[6], (H, DESTS), jnp.float32) ** block_scale(seeds[6], (H, DESTS), ((1, 8),), -0.2, 0.2)), 0.5, 2.0),
        "pair_share": jnp.clip(jnp.exp(jax.random.uniform(seeds[7], (DIST, DIST), jnp.float32, math.log(0.5), math.log(2.0))), 0.5, 2.0),
        "catchment": set_ends(ranked_ids(seeds[8], (ANCHORS // TB, DESTS // TB), LANES, 1), jax.random.fold_in(seeds[8], 3), 0, LANES - 1).astype(jnp.int32),
    }


def reference(anchor_coords, dest_coords, hour_decay, anchor_district, dest_district, anchor_target, dest_target, pair_share, catchment):
    sq_distance = (anchor_coords[0][:, None] - dest_coords[0][None, :]) ** 2 + (anchor_coords[1][:, None] - dest_coords[1][None, :]) ** 2
    dest_factor = jnp.ones((H, DESTS), jnp.float32)
    anchor_factor = jnp.ones((H, ANCHORS), jnp.float32)
    pair_factor = jnp.ones((DIST, DIST), jnp.float32)
    flow_scale = ANCHORS * H / (DIST * DIST)
    for sweep_index in range(SWEEPS):
        spread = pair_factor[anchor_district][:, dest_district]
        row_sums = jnp.stack([jnp.sum(jnp.exp(-hour_decay[hour] * sq_distance) * spread * dest_factor[hour][None, :], axis=1) for hour in range(H)])
        anchor_factor = anchor_target / row_sums
        col_sums = jnp.stack([jnp.sum(anchor_factor[hour][:, None] * jnp.exp(-hour_decay[hour] * sq_distance) * spread, axis=0) for hour in range(H)])
        dest_factor = dest_target / col_sums
        weight = jnp.zeros((ANCHORS, DESTS), jnp.float32)
        for hour in range(H):
            weight = weight + anchor_factor[hour][:, None] * jnp.exp(-hour_decay[hour] * sq_distance) * dest_factor[hour][None, :]
        by_anchor = jax.ops.segment_sum(weight, anchor_district, DIST)
        totals = jax.ops.segment_sum(by_anchor.T, dest_district, DIST).T
        pair_factor = pair_share * flow_scale / totals
    spread = pair_factor[anchor_district][:, dest_district]
    tile_list = []
    for hour in range(H):
        flows = anchor_factor[hour][:, None] * jnp.exp(-hour_decay[hour] * sq_distance) * dest_factor[hour][None, :] * spread
        tile_list.append(flows.reshape(ANCHORS // TB, TB, DESTS // TB, TB).sum(axis=(1, 3)).reshape(-1))
    tile_sums = jnp.stack(tile_list)
    lane_flows = jax.ops.segment_sum(tile_sums.T, catchment.reshape(-1), LANES).T
    return pair_factor, anchor_factor, dest_factor, lane_flows
```

```python
import functools

import jax
import jax.numpy as jnp
from jax import lax
from jax.experimental import pallas as pl
from jax.experimental.pallas import tpu as pltpu
from jax.sharding import PartitionSpec as P

TB = 8
LANE_DEV = 32
SWEEPS = 2
CH = 32
F32 = jnp.float32
BF16 = jnp.bfloat16


def nn(a, b):
    return lax.dot_general(a, b, (((1,), (0,)), ((), ())), preferred_element_type=F32)


def nt(a, b):
    return lax.dot_general(a, b, (((1,), (1,)), ((), ())), preferred_element_type=F32)


def split(x, parts):
    out = []
    for _ in range(parts):
        top = x.astype(BF16)
        out.append(top)
        x = x - top.astype(F32)
    return out


def iota(shape, axis):
    return lax.broadcasted_iota(jnp.int32, shape, axis)


def onehot(mask):
    return jnp.where(mask, 1.0, 0.0).astype(BF16)


def kernel(
    A, B, decay_ref, ac_ref, dc_ref, ad_ref, dd_ref, at_ref, dt_ref, share_ref, catch_ref,
    pf_out, a_out, b_out, lane_out,
    fa, fd, ta, td, pa, pd, seed, acc, u, spread, acol, colacc, rsum, csum,
    rbuf, cbuf, asnd, bsnd, abuf, bbuf, pfb, full, tsum, lanes, lbuf, lsum, mbuf,
    s_fa, r_fa, s_fd, r_fd, s_ta, r_ta, s_td, r_td, s_row, r_row, s_col, r_col,
    s_a, r_a, s_b, r_b, s_p1, r_p1, s_px, r_px, s_pc, r_pc, s_l, r_l, s_m, r_m,
):
    i = lax.axis_index("org")
    j = lax.axis_index("dst")
    N = ac_ref.shape[1]
    hours = at_ref.shape[0]
    districts = share_ref.shape[0]
    gd = districts // A
    kd = districts // B
    ra = N // gd
    rd = N // kd
    pack = 128 // kd
    scale = N * A * hours / (districts * districts)

    def remote(src, dst, ssem, rsem, org, dst_at):
        return pltpu.make_async_remote_copy(
            src_ref=src, dst_ref=dst, send_sem=ssem, recv_sem=rsem,
            device_id=(org, dst_at), device_id_type=pl.DeviceIdType.MESH)

    def exchange(axis, src_of, buf, ssem, rsem):
        me, n = (i, A) if axis == "org" else (j, B)
        sends = []
        for k in range(1, n):
            peer = lax.rem(me + k, n)
            dev = (peer, j) if axis == "org" else (i, peer)
            c = remote(src_of(peer), buf.at[me], ssem.at[k - 1], rsem.at[me], *dev)
            c.start()
            sends.append(c)

        def finish():
            for k in range(1, n):
                peer = lax.rem(me + k, n)
                dev = (peer, j) if axis == "org" else (i, peer)
                remote(buf.at[peer], buf.at[peer], ssem.at[k - 1], rsem.at[peer], *dev).wait_recv()
            for c in sends:
                c.wait_send()

        return finish

    def gathered(axis, value, buf, ssem, rsem):
        me = i if axis == "org" else j
        buf[me] = value
        return exchange(axis, lambda peer: buf.at[me], buf, ssem, rsem)

    def summed(buf, n):
        total = buf[0]
        for q in range(1, n):
            total = total + buf[q]
        return total

    barrier = pltpu.get_barrier_semaphore()
    for k in range(1, A):
        pl.semaphore_signal(barrier, inc=1, device_id=(lax.rem(i + k, A), j),
                            device_id_type=pl.DeviceIdType.MESH)
    for k in range(1, B):
        pl.semaphore_signal(barrier, inc=1, device_id=(i, lax.rem(j + k, B)),
                            device_id_type=pl.DeviceIdType.MESH)
    pl.semaphore_wait(barrier, A + B - 2)

    pad = jnp.zeros((5, N), F32)
    geo_a = jnp.concatenate([ac_ref[...], ad_ref[...].astype(F32), pad], axis=0)
    geo_d = jnp.concatenate([dc_ref[...], dd_ref[...].astype(F32), pad], axis=0)
    end_fd = gathered("dst", geo_d, fd, s_fd, r_fd)
    end_fa = gathered("org", geo_a, fa, s_fa, r_fa)
    end_td = gathered("dst", dt_ref[...], td, s_td, r_td)
    end_ta = gathered("org", at_ref[...], ta, s_ta, r_ta)

    before = onehot(iota((N, N), 0) < iota((N, N), 1))

    def place(feats, table, n, me, width, ranks):
        carry = jnp.zeros((width, 1), F32)
        for q in range(n):
            ids = feats[q, 2:3, :].astype(jnp.int32) - me * width
            mine = iota((width, N), 0) == ids
            flag = jnp.where(mine, 1.0, 0.0)
            count = nn(flag.astype(BF16), before) + carry
            carry = carry + jnp.sum(flag, axis=1, keepdims=True)
            for r in range(ranks):
                table[q, r * width:(r + 1) * width, :] = jnp.where(
                    count == r, flag, 0.0).astype(BF16)

    end_fa()
    place(fa, pa, A, i, gd, ra)
    acol_geo = jnp.zeros((N, 8), F32)
    for q in range(A):
        for part in split(fa[q], 3):
            acol_geo = acol_geo + nt(pa[q], part)
    acol[:, 0:8] = acol_geo
    end_fd()
    place(fd, pd, B, j, kd, rd)
    drow = jnp.zeros((8, N), F32)
    for q in range(B):
        for part in split(fd[q], 3):
            drow = drow + nt(part, pd[q])
    dx, dy = drow[0:1, :], drow[1:2, :]

    def fold(x):
        y = x[:, 0:128]
        for q in range(1, N // 128):
            y = y + x[:, q * 128:(q + 1) * 128]
        return y

    def seed_body(c, _):
        rows = pl.ds(pl.multiple_of(c * CH, CH), CH)
        xy = acol[rows, :]
        sq = (xy[:, 0:1] - dx) ** 2 + (xy[:, 1:2] - dy) ** 2
        for h in range(hours):
            s = jnp.exp(-decay_ref[h] * sq)
            seed[h, rows, :] = s
            acc[h, rows, :] = fold(s)
        return 0

    lax.fori_loop(0, N // CH, seed_body, 0)

    end_ta()
    end_td()
    a_target = jnp.zeros((8, N), F32)
    for q in range(A):
        for part in split(ta[q], 3):
            a_target = a_target + nt(part, pa[q])
    d_target = jnp.zeros((8, N), F32)
    for q in range(B):
        for part in split(td[q], 3):
            d_target = d_target + nt(part, pd[q])
    rsum[...] = a_target
    csum[...] = d_target

    eye = onehot(iota((N, N), 0) == iota((N, N), 1))
    pieces = []
    for q in range(pack):
        pieces.append(None)
    at_lane = pl.multiple_of(lax.div(j, pack) * 128, 128)
    wide = share_ref[pl.ds(pl.multiple_of(i * gd, gd), gd), pl.ds(at_lane, 128)]
    share = wide[:, 0:kd]
    for q in range(1, pack):
        share = jnp.where(lax.rem(j, pack) == q, wide[:, q * kd:(q + 1) * kd], share)

    dest = None
    for sweep in range(SWEEPS):
        if sweep > 0:
            def row_body(q, _):
                at = pl.multiple_of(q * CH, CH)
                sp = spread[pl.ds(at, CH), :]
                for h in range(hours):
                    sb = sp * dest[h:h + 1, :]
                    for r in range(ra):
                        rows = pl.ds(at + r * gd, CH)
                        acc[h, rows, :] = fold(seed[h, rows, :] * sb)
                return 0

            lax.fori_loop(0, gd // CH, row_body, 0)
        rows_sum = jnp.zeros((8, N), F32)
        for h in range(hours):
            pick = onehot(iota((8, 128), 0) == h)
            for part in split(acc[h], 2):
                rows_sum = rows_sum + nt(pick, part)
        gathered("dst", rows_sum, rbuf.at[sweep], s_row.at[sweep], r_row.at[sweep])()
        anchor = rsum[...] / summed(rbuf.at[sweep], B)
        parts = split(anchor, 3)
        acol[:, 0:8] = nt(eye, parts[0]) + nt(eye, parts[1]) + nt(eye, parts[2])
        if sweep == SWEEPS - 1:
            for q in range(A):
                asnd[q] = nn(parts[0], pa[q]) + nn(parts[1], pa[q]) + nn(parts[2], pa[q])
            abuf[i] = asnd[i]
            end_a = exchange("org", lambda peer: asnd.at[peer], abuf, s_a, r_a)
        colacc[...] = jnp.zeros_like(colacc)

        def col_body(q, _):
            at = pl.multiple_of(q * CH, CH)
            for h in range(hours):
                t = None
                for r in range(ra):
                    rows = pl.ds(at + r * gd, CH)
                    term = acol[rows, h:h + 1] * seed[h, rows, :]
                    t = term if t is None else t + term
                u[h, pl.ds(at, CH), :] = t
                if sweep > 0:
                    t = t * spread[pl.ds(at, CH), :]
                colacc[h] = colacc[h] + jnp.sum(t.reshape(CH // 8, 8, N), axis=0)
            return 0

        lax.fori_loop(0, gd // CH, col_body, 0)
        cols_sum = jnp.concatenate(
            [jnp.sum(colacc[h], axis=0, keepdims=True) for h in range(hours)], axis=0)
        gathered("org", cols_sum, cbuf.at[sweep], s_col.at[sweep], r_col.at[sweep])()
        dest = csum[...] / summed(cbuf.at[sweep], A)
        if sweep == SWEEPS - 1:
            parts = split(dest, 3)
            for q in range(B):
                bsnd[q] = nn(parts[0], pd[q]) + nn(parts[1], pd[q]) + nn(parts[2], pd[q])
            bbuf[j] = bsnd[j]
            end_b = exchange("dst", lambda peer: bsnd.at[peer], bbuf, s_b, r_b)

        def total_body(q, _):
            rows = pl.ds(pl.multiple_of(q * CH, CH), CH)
            t = u[0, rows, :] * dest[0:1, :]
            for h in range(1, hours):
                t = t + u[h, rows, :] * dest[h:h + 1, :]
            acc[0, rows, :] = fold(t)
            return 0

        lax.fori_loop(0, gd // CH, total_body, 0)
        folded = acc[0, 0:gd, :]
        totals = folded[:, 0:kd]
        for q in range(1, pack):
            totals = totals + folded[:, q * kd:(q + 1) * kd]
        pair = share * scale / totals
        if sweep < SWEEPS - 1:
            spread[...] = jnp.concatenate([pair] * rd, axis=1)

    ph = gd // pack
    pfb[i, j] = jnp.concatenate([pair[q * ph:(q + 1) * ph, :] for q in range(pack)], axis=1)
    core = lax.rem(i, 2)
    X = A // 2
    sib = i + 1 - 2 * core
    pending = []
    for k in range(1, B):
        c = remote(pfb.at[i, j], pfb.at[i, j], s_p1.at[k - 1], r_p1.at[j], i, lax.rem(j + k, B))
        c.start()
        pending.append(c)

    def spread_x(b):
        for k in range(1, X):
            to = lax.rem(i + 2 * k, A)
            c = remote(pfb.at[i, b], pfb.at[i, b], s_px.at[k - 1, b], r_px.at[k - 1, b], to, j)
            c.start()
            pending.append(c)

    def to_core(g, b, slot):
        c = remote(pfb.at[g, b], pfb.at[g, b], s_pc.at[slot, b], r_pc.at[slot, b], sib, j)
        c.start()
        pending.append(c)

    spread_x(j)
    to_core(i, j, 0)

    o = iota((N, N), 0)
    half = N // TB // 2
    r_of = lax.div(o, 2 * half)
    e_of = lax.rem(lax.div(o, half), 2)
    p_of = lax.rem(o, half)
    order = onehot(iota((N, N), 1) == (2 * p_of + e_of) * TB + r_of)
    own = jnp.zeros((N, 8), F32)
    for part in split(geo_a, 3):
        own = own + nt(order, part)
    end_a()
    end_b()
    a_own = summed(abuf, A)
    b_own = summed(bbuf, B)
    a_out[...] = a_own
    b_out[...] = b_own
    parts = split(a_own, 3)
    acol[:, 0:8] = nt(order, parts[0]) + nt(order, parts[1]) + nt(order, parts[2])
    acol[:, 8:16] = own
    ex, ey = dc_ref[0:1, :], dc_ref[1:2, :]

    def flow_body(c, _):
        rows = pl.ds(pl.multiple_of(c * CH, CH), CH)
        col = acol[rows, :]
        sq = (col[:, 8:9] - ex) ** 2 + (col[:, 9:10] - ey) ** 2
        for h in range(hours):
            seed[h, rows, :] = col[:, h:h + 1] * jnp.exp(-decay_ref[h] * sq) * b_own[h:h + 1, :]
        return 0

    def recv(g, b, sem):
        remote(pfb.at[g, b], pfb.at[g, b], s_p1.at[0], sem, sib, j).wait_recv()

    steps = N // CH
    lax.fori_loop(0, steps // 2, flow_body, 0)
    for k in range(1, B):
        b = lax.rem(j + k, B)
        recv(i, b, r_p1.at[b])
        spread_x(b)
        to_core(i, b, 0)
    lax.fori_loop(steps // 2, steps, flow_body, 0)
    for k in range(1, X):
        g = lax.rem(i + A - 2 * k, A)
        for m in range(B):
            b = lax.rem(j + m, B)
            recv(g, b, r_px.at[k - 1, b])
            to_core(g, b, k)
    left = onehot(own[:, 2:3].astype(jnp.int32) == iota((N, districts), 1))
    right = onehot(iota((districts, N), 0) == dd_ref[...])
    for k in range(X):
        g = lax.rem(sib + A - 2 * k, A)
        for m in range(B):
            b = lax.rem(j + m, B)
            recv(g, b, r_pc.at[k, b])
    for c in pending:
        c.wait_send()

    for g in range(A):
        for q in range(pack):
            full[g * gd + q * ph:g * gd + (q + 1) * ph, :] = jnp.concatenate(
                [pfb[g, b, :, q * kd:(q + 1) * kd] for b in range(B)], axis=1)
    pf_out[...] = full[...]
    high, low = split(full[...], 2)
    full[...] = nn(nn(left, high).astype(BF16), right) + nn(nn(left, low).astype(BF16), right)

    tiles = N // TB

    def tile_body(c, _):
        at = pl.multiple_of(c * 16, 16)
        for h in range(hours):
            t = None
            for r in range(TB):
                rows = pl.ds(at + r * tiles, 16)
                term = seed[h, rows, :] * full[rows, :]
                t = term if t is None else t + term
            acc[h, pl.ds(at, 16), :] = t[:, 0:128]
            for q in range(1, N // 128):
                acc[h, pl.ds(at + q * tiles, 16), :] = t[:, q * 128:(q + 1) * 128]
        return 0

    lax.fori_loop(0, tiles // 16, tile_body, 0)
    for h in range(hours):
        pair_sum = jnp.zeros((half, 128), F32)
        for q in range(N // 128):
            for e in range(2):
                at = q * tiles + e * half
                pool = onehot(lax.div(iota((128, 128), 0), TB) + q * (128 // TB) + e * tiles
                              == iota((128, 128), 1))
                for part in split(acc[h, at:at + half, :], 2):
                    pair_sum = pair_sum + nn(part, pool)
        tsum[h] = pair_sum

    slabs = lanes.shape[0]
    result = jnp.zeros((slabs * 8, 128), F32)
    slab_of = lax.div(iota((slabs * 8, 128), 0), 8)
    for p in range(half):
        ids = catch_ref[p:p + 1, :]
        top = lax.div(ids, 128)
        low_of = ids - top * 128
        t = tsum[:, p, :]
        t = jnp.concatenate([t] * slabs, axis=0)
        t = jnp.where(slab_of == top, t, 0.0)
        lo = onehot(iota((128, 128), 0) == low_of)
        for part in split(t, 2):
            result = result + nt(part, lo)
    lanes[...] = result.reshape(slabs, 8, 128)

    per = slabs // A
    lbuf[i] = lanes[pl.ds(i * per, per)]
    exchange("org", lambda peer: lanes.at[pl.ds(peer * per, per)], lbuf, s_l, r_l)()
    lsum[...] = summed(lbuf, A)
    share_of = 128 // LANE_DEV
    mbuf[j] = lsum[lax.div(j, share_of)]
    exchange("dst", lambda peer: lsum.at[lax.div(peer, share_of)], mbuf, s_m, r_m)()
    total = summed(mbuf, B)
    mine = total[:, 0:LANE_DEV]
    for q in range(1, share_of):
        mine = jnp.where(lax.rem(j, share_of) == q,
                         total[:, q * LANE_DEV:(q + 1) * LANE_DEV], mine)
    lane_out[...] = mine


def per_device(
    anchor_coords, dest_coords, hour_decay, anchor_district, dest_district,
    anchor_target, dest_target, pair_share, catchment,
):
    A = lax.axis_size("org")
    B = lax.axis_size("dst")
    N = anchor_coords.shape[1]
    hours = hour_decay.shape[0]
    districts = pair_share.shape[0]
    gd, kd = districts // A, districts // B
    ph = gd // (128 // kd)
    slabs = LANE_DEV * A * B // 128
    V = pltpu.VMEM
    dma = pltpu.SemaphoreType.DMA
    scratch = [
        V((A, 8, N), F32), V((B, 8, N), F32), V((A, 8, N), F32), V((B, 8, N), F32),
        V((A, N, N), BF16), V((B, N, N), BF16),
        V((hours, N, N), F32), V((hours, N, 128), F32), V((hours, gd, N), F32),
        V((gd, N), F32), V((N, 128), F32), V((hours, 8, N), F32),
        V((8, N), F32), V((8, N), F32),
        V((SWEEPS, B, 8, N), F32), V((SWEEPS, A, 8, N), F32),
        V((A, 8, N), F32), V((B, 8, N), F32), V((A, 8, N), F32), V((B, 8, N), F32),
        V((A, B, ph, 128), F32), V((districts, districts), F32),
        V((hours, N // TB // 2, 128), F32), V((slabs, 8, 128), F32),
        V((A, slabs // A, 8, 128), F32), V((slabs // A, 8, 128), F32), V((B, 8, 128), F32),
    ]
    X = A // 2
    for shape in (
        (A,), (A,), (B,), (B,), (A,), (A,), (B,), (B,),
        (SWEEPS, B), (SWEEPS, B), (SWEEPS, A), (SWEEPS, A),
        (A,), (A,), (B,), (B,), (B,), (B,),
        (max(X - 1, 1), B), (max(X - 1, 1), B), (X, B), (X, B),
        (A,), (A,), (B,), (B,),
    ):
        scratch.append(dma(shape))
    vm = pl.BlockSpec(memory_space=pltpu.VMEM)
    return tuple(pl.pallas_call(
        functools.partial(kernel, A, B),
        out_shape=(
            jax.ShapeDtypeStruct((districts, districts), F32),
            jax.ShapeDtypeStruct((hours, N), F32),
            jax.ShapeDtypeStruct((hours, N), F32),
            jax.ShapeDtypeStruct((hours, LANE_DEV), F32),
        ),
        in_specs=[pl.BlockSpec(memory_space=pltpu.SMEM)] + [vm] * 8,
        out_specs=(vm, vm, vm, vm),
        scratch_shapes=scratch,
        compiler_params=pltpu.CompilerParams(
            collective_id=0, has_side_effects=True, vmem_limit_bytes=56 * 1024 * 1024),
    )(
        hour_decay, anchor_coords, dest_coords,
        anchor_district.reshape(1, N), dest_district.reshape(1, N),
        anchor_target, dest_target, pair_share,
        catchment.reshape(N // TB // 2, 128),
    ))


def solution(mesh):
    return jax.shard_map(
        per_device,
        mesh=mesh,
        in_specs=(
            P(None, "org"), P(None, "dst"), P(), P("org"), P("dst"),
            P(None, "org"), P(None, "dst"), P(), P("org", "dst"),
        ),
        out_specs=(P(), P(None, "org"), P(None, "dst"), P(None, ("org", "dst"))),
        check_vma=False,
    )
```

```python
import functools

import jax
import jax.numpy as jnp
from jax import lax
from jax.experimental import pallas as pl
from jax.experimental.pallas import tpu as pltpu
from jax.sharding import PartitionSpec as P

TB = 8
LANE_DEV = 32
SWEEPS = 2
CH = 32
F32 = jnp.float32
BF16 = jnp.bfloat16


def nn(a, b):
    return lax.dot_general(a, b, (((1,), (0,)), ((), ())), preferred_element_type=F32)


def nt(a, b):
    return lax.dot_general(a, b, (((1,), (1,)), ((), ())), preferred_element_type=F32)


def split(x, parts):
    out = []
    for _ in range(parts):
        top = x.astype(BF16)
        out.append(top)
        x = x - top.astype(F32)
    return out


def iota(shape, axis):
    return lax.broadcasted_iota(jnp.int32, shape, axis)


def stacked(x, parts):
    return jnp.concatenate([p.astype(F32) for p in split(x, parts)], axis=0).astype(BF16)


def rows_added(y):
    return y[0:8] + y[8:16] + y[16:24]


def cols_added(y):
    return y[:, 0:8] + y[:, 8:16] + y[:, 16:24]


def onehot(mask):
    return jnp.where(mask, 1.0, 0.0).astype(BF16)


def kernel(
    A, B, decay_ref, ac_ref, dc_ref, ad_ref, dd_ref, at_ref, dt_ref, share_ref, catch_ref,
    pf_out, a_out, b_out, lane_out,
    fa, fd, ta, td, pa, pd, seed, acc, u, spread, acol, colacc,
    rbuf, cbuf, asnd, bsnd, abuf, bbuf, pfb, full, mixed, tsum, lanes, lbuf, lsum, mbuf,
    share_in, by_slab, by_low, s_share, s_pf,
    s_fa, r_fa, s_fd, r_fd, s_ta, r_ta, s_td, r_td, s_row, r_row, s_col, r_col,
    s_a, r_a, s_b, r_b, s_p1, r_p1, s_px, r_px, s_pc, r_pc, s_l, r_l, s_m, r_m,
):
    i = lax.axis_index("org")
    j = lax.axis_index("dst")
    N = ac_ref.shape[1]
    hours = at_ref.shape[0]
    districts = share_ref.shape[0]
    gd = districts // A
    kd = districts // B
    ra = N // gd
    rd = N // kd
    pack = 128 // kd
    scale = N * A * hours / (districts * districts)

    def remote(src, dst, ssem, rsem, org, dst_at):
        return pltpu.make_async_remote_copy(
            src_ref=src, dst_ref=dst, send_sem=ssem, recv_sem=rsem,
            device_id=(org, dst_at), device_id_type=pl.DeviceIdType.MESH)

    def exchange(axis, src_of, buf, ssem, rsem):
        me, n = (i, A) if axis == "org" else (j, B)
        sends = []
        for k in range(1, n):
            peer = lax.rem(me + k, n)
            dev = (peer, j) if axis == "org" else (i, peer)
            c = remote(src_of(peer), buf.at[me], ssem.at[k - 1], rsem.at[me], *dev)
            c.start()
            sends.append(c)

        def finish():
            for k in range(1, n):
                peer = lax.rem(me + k, n)
                dev = (peer, j) if axis == "org" else (i, peer)
                remote(buf.at[peer], buf.at[peer], ssem.at[k - 1], rsem.at[peer], *dev).wait_recv()
            for c in sends:
                c.wait_send()

        return finish

    def gathered(axis, value, buf, ssem, rsem):
        me = i if axis == "org" else j
        buf[me] = value
        return exchange(axis, lambda peer: buf.at[me], buf, ssem, rsem)

    def summed(buf, n):
        total = buf[0]
        for q in range(1, n):
            total = total + buf[q]
        return total

    at_lane = pl.multiple_of(lax.div(j, pack) * 128, 128)
    share_copy = pltpu.make_async_copy(
        share_ref.at[pl.ds(pl.multiple_of(i * gd, gd), gd), pl.ds(at_lane, 128)],
        share_in, s_share)
    share_copy.start()
    barrier = pltpu.get_barrier_semaphore()
    for k in range(1, A):
        pl.semaphore_signal(barrier, inc=1, device_id=(lax.rem(i + k, A), j),
                            device_id_type=pl.DeviceIdType.MESH)
    for k in range(1, B):
        pl.semaphore_signal(barrier, inc=1, device_id=(i, lax.rem(j + k, B)),
                            device_id_type=pl.DeviceIdType.MESH)
    pl.semaphore_wait(barrier, A + B - 2)

    pad = jnp.zeros((5, N), F32)
    geo_a = jnp.concatenate([ac_ref[...], ad_ref[...].astype(F32), pad], axis=0)
    geo_d = jnp.concatenate([dc_ref[...], dd_ref[...].astype(F32), pad], axis=0)
    end_fd = gathered("dst", geo_d, fd, s_fd, r_fd)
    end_fa = gathered("org", geo_a, fa, s_fa, r_fa)
    end_td = gathered("dst", dt_ref[...], td, s_td, r_td)
    end_ta = gathered("org", at_ref[...], ta, s_ta, r_ta)

    before = onehot(iota((N, N), 0) < iota((N, N), 1))

    def place(feats, table, n, me, width, ranks):
        flags = []
        for q in range(n):
            ids = feats[q, 2:3, :].astype(jnp.int32) - me * width
            flags.append(jnp.where(iota((width, N), 0) == ids, 1.0, 0.0))
        counts = nn(jnp.concatenate(flags, axis=0).astype(BF16), before)
        carry = jnp.zeros((width, 1), F32)
        for q in range(n):
            flag = flags[q]
            count = counts[q * width:(q + 1) * width, :] + carry
            carry = count[:, N - 1:N] + flag[:, N - 1:N]
            for r in range(ranks):
                table[q, r * width:(r + 1) * width, :] = jnp.where(
                    count == r, flag, 0.0).astype(BF16)

    def to_slots(feats, table, n):
        y = jnp.zeros((24, N), F32)
        for q in range(n):
            y = y + nt(stacked(feats[q], 3), table[q])
        return rows_added(y)

    end_fa()
    place(fa, pa, A, i, gd, ra)
    geo = jnp.zeros((N, 24), F32)
    for q in range(A):
        geo = geo + nt(pa[q], stacked(fa[q], 3))
    acol[:, 0:8] = cols_added(geo)
    end_fd()
    place(fd, pd, B, j, kd, rd)
    drow = to_slots(fd, pd, B)
    dx, dy = drow[0:1, :], drow[1:2, :]

    def fold(x):
        y = x[:, 0:128]
        for q in range(1, N // 128):
            y = y + x[:, q * 128:(q + 1) * 128]
        return y

    def seed_body(c, _):
        rows = pl.ds(pl.multiple_of(c * CH, CH), CH)
        xy = acol[rows, :]
        sq = (xy[:, 0:1] - dx) ** 2 + (xy[:, 1:2] - dy) ** 2
        for h in range(hours):
            s = jnp.exp(-decay_ref[h] * sq)
            seed[h, rows, :] = s
            acc[h, rows, :] = fold(s)
        return 0

    lax.fori_loop(0, N // CH, seed_body, 0)

    dest = None
    a_target = d_target = share = None
    for sweep in range(SWEEPS):
        if sweep > 0:
            def row_body(q, _):
                at = pl.multiple_of(q * CH, CH)
                sp = spread[pl.ds(at, CH), :]
                for h in range(hours):
                    sb = sp * dest[h:h + 1, :]
                    for r in range(ra):
                        rows = pl.ds(at + r * gd, CH)
                        acc[h, rows, :] = fold(seed[h, rows, :] * sb)
                return 0

            lax.fori_loop(0, gd // CH, row_body, 0)
        rows_sum = jnp.zeros((8, N), F32)
        for h in range(hours):
            pick = onehot(iota((8, 128), 0) == h)
            for part in split(acc[h], 2):
                rows_sum = rows_sum + nt(pick, part)
        end_row = gathered("dst", rows_sum, rbuf.at[sweep], s_row.at[sweep], r_row.at[sweep])
        if sweep == 0:
            end_ta()
            a_target = to_slots(ta, pa, A)
            end_td()
            d_target = to_slots(td, pd, B)
            share_copy.wait()
            share = share_in[:, 0:kd]
            for q in range(1, pack):
                share = jnp.where(lax.rem(j, pack) == q, share_in[:, q * kd:(q + 1) * kd], share)
        end_row()
        anchor = a_target / summed(rbuf.at[sweep], B)
        acol[:, 0:8] = anchor.T
        colacc[...] = jnp.zeros_like(colacc)

        def col_body(q, _):
            at = pl.multiple_of(q * CH, CH)
            for h in range(hours):
                t = None
                for r in range(ra):
                    rows = pl.ds(at + r * gd, CH)
                    term = acol[rows, h:h + 1] * seed[h, rows, :]
                    t = term if t is None else t + term
                u[h, pl.ds(at, CH), :] = t
                if sweep > 0:
                    t = t * spread[pl.ds(at, CH), :]
                colacc[h] = colacc[h] + jnp.sum(t.reshape(CH // 8, 8, N), axis=0)
            return 0

        lax.fori_loop(0, gd // CH, col_body, 0)
        cols_sum = jnp.concatenate(
            [jnp.sum(colacc[h], axis=0, keepdims=True) for h in range(hours)], axis=0)
        end_col = gathered("org", cols_sum, cbuf.at[sweep], s_col.at[sweep], r_col.at[sweep])
        if sweep == SWEEPS - 1:
            parts = stacked(anchor, 3)
            for q in range(A):
                asnd[q] = rows_added(nn(parts, pa[q]))
            abuf[i] = asnd[i]
            end_a = exchange("org", lambda peer: asnd.at[peer], abuf, s_a, r_a)
        end_col()
        dest = d_target / summed(cbuf.at[sweep], A)

        def total_body(q, _):
            rows = pl.ds(pl.multiple_of(q * CH, CH), CH)
            t = u[0, rows, :] * dest[0:1, :]
            for h in range(1, hours):
                t = t + u[h, rows, :] * dest[h:h + 1, :]
            acc[0, rows, :] = fold(t)
            return 0

        lax.fori_loop(0, gd // CH, total_body, 0)
        folded = acc[0, 0:gd, :]
        totals = folded[:, 0:kd]
        for q in range(1, pack):
            totals = totals + folded[:, q * kd:(q + 1) * kd]
        pair = share * scale / totals
        if sweep < SWEEPS - 1:
            spread[...] = jnp.concatenate([pair] * rd, axis=1)

    ph = gd // pack
    pfb[i, j] = jnp.concatenate([pair[q * ph:(q + 1) * ph, :] for q in range(pack)], axis=1)
    core = lax.rem(i, 2)
    X = A // 2
    sib = i + 1 - 2 * core
    pending = []
    for k in range(1, B):
        c = remote(pfb.at[i, j], pfb.at[i, j], s_p1.at[k - 1], r_p1.at[j], i, lax.rem(j + k, B))
        c.start()
        pending.append(c)

    def spread_x(b):
        for k in range(1, X):
            to = lax.rem(i + 2 * k, A)
            c = remote(pfb.at[i, b], pfb.at[i, b], s_px.at[k - 1, b], r_px.at[k - 1, b], to, j)
            c.start()
            pending.append(c)

    def to_core(g, b, slot):
        c = remote(pfb.at[g, b], pfb.at[g, b], s_pc.at[slot, b], r_pc.at[slot, b], sib, j)
        c.start()
        pending.append(c)

    spread_x(j)
    to_core(i, j, 0)

    parts = stacked(dest, 3)
    for q in range(B):
        bsnd[q] = rows_added(nn(parts, pd[q]))
    bbuf[j] = bsnd[j]
    end_b = exchange("dst", lambda peer: bsnd.at[peer], bbuf, s_b, r_b)

    o = iota((N, N), 0)
    half = N // TB // 2
    r_of = lax.div(o, 2 * half)
    e_of = lax.rem(lax.div(o, half), 2)
    p_of = lax.rem(o, half)
    order = onehot(iota((N, N), 1) == (2 * p_of + e_of) * TB + r_of)
    own = cols_added(nt(order, stacked(geo_a, 3)))
    end_a()
    end_b()
    a_own = summed(abuf, A)
    b_own = summed(bbuf, B)
    a_out[...] = a_own
    b_out[...] = b_own
    acol[:, 0:8] = cols_added(nt(order, stacked(a_own, 3)))
    acol[:, 8:16] = own
    ex, ey = dc_ref[0:1, :], dc_ref[1:2, :]

    def flow_body(c, _):
        rows = pl.ds(pl.multiple_of(c * CH, CH), CH)
        col = acol[rows, :]
        sq = (col[:, 8:9] - ex) ** 2 + (col[:, 9:10] - ey) ** 2
        for h in range(hours):
            seed[h, rows, :] = col[:, h:h + 1] * jnp.exp(-decay_ref[h] * sq) * b_own[h:h + 1, :]
        return 0

    def recv(g, b, sem):
        remote(pfb.at[g, b], pfb.at[g, b], s_p1.at[0], sem, sib, j).wait_recv()

    steps = N // CH
    for k in range(1, B):
        b = lax.rem(j + k, B)
        recv(i, b, r_p1.at[b])
        spread_x(b)
        to_core(i, b, 0)
    lax.fori_loop(0, steps // 2, flow_body, 0)
    for k in range(1, X):
        g = lax.rem(i + A - 2 * k, A)
        for m in range(B):
            b = lax.rem(j + m, B)
            recv(g, b, r_px.at[k - 1, b])
            to_core(g, b, k)
    lax.fori_loop(steps // 2, steps, flow_body, 0)
    even = catch_ref[pl.ds(0, half, stride=2), :]
    odd = catch_ref[pl.ds(1, half, stride=2), :]
    catch = jnp.concatenate([even, odd], axis=1)
    catch_top = lax.div(catch, 128)
    catch_low = catch - catch_top * 128
    for p in range(half):
        by_low[:, p * 128:(p + 1) * 128] = onehot(iota((128, 128), 0) == catch_low[p:p + 1, :])
    left = onehot(own[:, 2:3].astype(jnp.int32) == iota((N, districts), 1))
    right = onehot(iota((districts, N), 0) == dd_ref[...])
    for k in range(X):
        g = lax.rem(sib + A - 2 * k, A)
        for m in range(B):
            b = lax.rem(j + m, B)
            recv(g, b, r_pc.at[k, b])
    for c in pending:
        c.wait_send()

    for g in range(A):
        for q in range(pack):
            full[g * gd + q * ph:g * gd + (q + 1) * ph, :] = jnp.concatenate(
                [pfb[g, b, :, q * kd:(q + 1) * kd] for b in range(B)], axis=1)
    pf_copy = pltpu.make_async_copy(full, pf_out, s_pf)
    pf_copy.start()
    high, low = split(full[...], 2)
    mixed[...] = nn(nn(left, high).astype(BF16), right) + nn(nn(left, low).astype(BF16), right)

    tiles = N // TB

    def tile_body(c, _):
        at = pl.multiple_of(c * 16, 16)
        for h in range(hours):
            t = None
            for r in range(TB):
                rows = pl.ds(at + r * tiles, 16)
                term = seed[h, rows, :] * mixed[rows, :]
                t = term if t is None else t + term
            u[h, pl.ds(at, 16), :] = t
        return 0

    lax.fori_loop(0, tiles // 16, tile_body, 0)
    pair_sum = jnp.zeros((hours * half, 128), F32)
    for e in range(2):
        pool = onehot(lax.div(iota((N, 128), 0), TB) + e * tiles == iota((N, 128), 1))
        for part in split(u[:, e * half:(e + 1) * half, :].reshape(hours * half, N), 2):
            pair_sum = pair_sum + nn(part, pool)
    tsum[...] = pair_sum.reshape(hours, half, 128)

    slabs = lanes.shape[0]
    slab_of = lax.div(iota((slabs * 8, 128), 0), 8)
    for p in range(half):
        t = jnp.concatenate([tsum[:, p, :]] * slabs, axis=0)
        t = jnp.where(slab_of == catch_top[p:p + 1, :], t, 0.0)
        for m, part in enumerate(split(t, 2)):
            by_slab[m * slabs * 8:(m + 1) * slabs * 8, p * 128:(p + 1) * 128] = part
    result = nt(by_slab[...], by_low[...])
    result = result[0:slabs * 8] + result[slabs * 8:]
    lanes[...] = result.reshape(slabs, 8, 128)

    per = slabs // A
    lbuf[i] = lanes[pl.ds(i * per, per)]
    exchange("org", lambda peer: lanes.at[pl.ds(peer * per, per)], lbuf, s_l, r_l)()
    lsum[...] = summed(lbuf, A)
    share_of = 128 // LANE_DEV
    mbuf[j] = lsum[lax.div(j, share_of)]
    exchange("dst", lambda peer: lsum.at[lax.div(peer, share_of)], mbuf, s_m, r_m)()
    total = summed(mbuf, B)
    mine = total[:, 0:LANE_DEV]
    for q in range(1, share_of):
        mine = jnp.where(lax.rem(j, share_of) == q,
                         total[:, q * LANE_DEV:(q + 1) * LANE_DEV], mine)
    lane_out[...] = mine
    pf_copy.wait()


def per_device(
    anchor_coords, dest_coords, hour_decay, anchor_district, dest_district,
    anchor_target, dest_target, pair_share, catchment,
):
    A = lax.axis_size("org")
    B = lax.axis_size("dst")
    N = anchor_coords.shape[1]
    hours = hour_decay.shape[0]
    districts = pair_share.shape[0]
    gd, kd = districts // A, districts // B
    ph = gd // (128 // kd)
    slabs = LANE_DEV * A * B // 128
    V = pltpu.VMEM
    dma = pltpu.SemaphoreType.DMA
    scratch = [
        V((A, 8, N), F32), V((B, 8, N), F32), V((A, 8, N), F32), V((B, 8, N), F32),
        V((A, N, N), BF16), V((B, N, N), BF16),
        V((hours, N, N), F32), V((hours, N, 128), F32), V((hours, gd, N), F32),
        V((gd, N), F32), V((N, 128), F32), V((hours, 8, N), F32),
        V((SWEEPS, B, 8, N), F32), V((SWEEPS, A, 8, N), F32),
        V((A, 8, N), F32), V((B, 8, N), F32), V((A, 8, N), F32), V((B, 8, N), F32),
        V((A, B, ph, 128), F32), V((districts, districts), F32), V((N, N), F32),
        V((hours, N // TB // 2, 128), F32), V((slabs, 8, 128), F32),
        V((A, slabs // A, 8, 128), F32), V((slabs // A, 8, 128), F32), V((B, 8, 128), F32),
        V((gd, 128), F32), V((slabs * 16, N // TB * (N // TB)), BF16),
        V((128, N // TB * (N // TB)), BF16), dma(()), dma(()),
    ]
    X = A // 2
    for shape in (
        (A,), (A,), (B,), (B,), (A,), (A,), (B,), (B,),
        (SWEEPS, B), (SWEEPS, B), (SWEEPS, A), (SWEEPS, A),
        (A,), (A,), (B,), (B,), (B,), (B,),
        (max(X - 1, 1), B), (max(X - 1, 1), B), (X, B), (X, B),
        (A,), (A,), (B,), (B,),
    ):
        scratch.append(dma(shape))
    vm = pl.BlockSpec(memory_space=pltpu.VMEM)
    anywhere = pl.BlockSpec(memory_space=pl.ANY)
    return tuple(pl.pallas_call(
        functools.partial(kernel, A, B),
        out_shape=(
            jax.ShapeDtypeStruct((districts, districts), F32),
            jax.ShapeDtypeStruct((hours, N), F32),
            jax.ShapeDtypeStruct((hours, N), F32),
            jax.ShapeDtypeStruct((hours, LANE_DEV), F32),
        ),
        in_specs=[pl.BlockSpec(memory_space=pltpu.SMEM)] + [vm] * 6 + [anywhere, vm],
        out_specs=(anywhere, vm, vm, vm),
        scratch_shapes=scratch,
        compiler_params=pltpu.CompilerParams(
            collective_id=0, has_side_effects=True, vmem_limit_bytes=56 * 1024 * 1024),
    )(
        hour_decay, anchor_coords, dest_coords,
        anchor_district.reshape(1, N), dest_district.reshape(1, N),
        anchor_target, dest_target, pair_share,
        catchment,
    ))


def solution(mesh):
    return jax.shard_map(
        per_device,
        mesh=mesh,
        in_specs=(
            P(None, "org"), P(None, "dst"), P(), P("org"), P("dst"),
            P(None, "org"), P(None, "dst"), P(), P("org", "dst"),
        ),
        out_specs=(P(), P(None, "org"), P(None, "dst"), P(None, ("org", "dst"))),
        check_vma=False,
    )
```
